32 devices in a mesh: parts: 2 (over y), blk: 8 (over z, x), ugrp: 2 (over core).
Axes of the slice: x: 2, y: 2, z: 4, core: 2. Of those that a mesh axis runs over, the one named last changes fastest.
Arguments:
- rating_tiles: bfloat16 [32768, 4, 256], P(('parts', 'blk', 'ugrp')), parts along dimension 0, may hold values from -6 to 6
- tile_mask: int32 [32768, 4, 256], P(('parts', 'blk', 'ugrp')), parts along dimension 0, may hold values 0 or 1
- user_rows: float32 [32768, 256], P(('parts', 'blk', 'ugrp')), parts along dimension 0, may hold values from -1.5 to 1.5
- item_rows: float32 [4096, 256], P(('parts', 'blk', 'ugrp')), parts along dimension 0, may hold values from -1.5 to 1.5
- user_noise: bfloat16 [2, 32768, 256], P(None, ('parts', 'blk', 'ugrp')), parts along dimension 1, may hold values from -6 to 6
- item_noise: bfloat16 [2, 4096, 256], P(None, ('parts', 'blk', 'ugrp')), parts along dimension 1, may hold values from -6 to 6
Outputs:
- new_users: float32 [32768, 256], P(('parts', 'blk', 'ugrp')), parts along dimension 0
- new_items: float32 [4096, 256], P(('parts', 'blk', 'ugrp')), parts along dimension 0
The draws below stay inside these ranges and needn't reach their ends.
There are 2 independent parts, one for each index of `parts`. The reference program is written for one: setup_inputs(seed, part) draws one part's arguments, and reference() takes and returns one part's arrays. A program takes and returns all parts, laid end to end along the dimension named above; each array names one. Nothing has to cross between parts.
All inputs are finite; a program needn't handle non-finite values. No bound on the sum of `tile_mask` on one device may be relied on, other than what follows from the above.
Results may differ from the reference program's by a relative error of at most 0.0085.
Values may be sent and summed in bfloat16 or wider, within the bound.
A program may use at most 64 MiB of HBM per device.

```python
import math
import jax
import jax.numpy as jnp
from jax import lax

R = 256
IB = 256
ROUNDS = 4
ITERS = 2
GROUP_ROWS = 2048
USERS = 16384
ITEMS = 2048


def touch_ends(drawn, key, low, largest):
    dims = drawn.shape
    place = [jax.random.randint(jax.random.fold_in(key, axis), (), 0, dims[axis]) for axis in range(len(dims))]
    drawn = drawn.at[tuple(place)].set(low)
    longest = dims.index(max(dims))
    place[longest] = (place[longest] + 1) % dims[longest]
    return drawn.at[tuple(place)].set(largest)


def levels(key, extent, cuts, smallest, high):
    factor_of, own = 1.0, jax.random.fold_in(key, 6)
    for position, shards_of in cuts:
        steps = jnp.exp(jax.random.uniform(jax.random.fold_in(own, position), (shards_of,), jnp.float32, smallest / len(cuts), high / len(cuts)))
        factor_of = factor_of * jnp.repeat(steps, extent[position] // shards_of).reshape([-1 if axis == position else 1 for axis in range(len(extent))])
    return factor_of


def bell_draw(key, dims, width, bound, pieces=(), held_as=jnp.bfloat16):
    entries = jax.random.normal(key, dims, jnp.float32) * width
    if len(pieces) > 0:
        entries = levels(key, dims, pieces, -0.22, 0.18) * entries
    return jnp.clip(entries, min=-bound, max=bound).astype(held_as)


def setup_inputs(seed: int = 0, part: int = 0) -> dict:
    key_of = jax.random.split(jax.random.key(seed), 7)
    part_splits = jax.random.split(jax.random.fold_in(key_of[6], part), 7)
    rating_tiles = bell_draw(part_splits[0], (USERS, ROUNDS, IB), 1.0, 6.0, ((0, 16),))
    tile_mask = touch_ends((jax.random.randint(part_splits[1], (USERS, ROUNDS, IB), 0, 2) < 1).astype(jnp.int32), jax.random.fold_in(part_splits[1], 1), 0, 1)
    user_rows = bell_draw(part_splits[2], (USERS, R), 0.25, 1.5, ((0, 16),), jnp.float32)
    item_rows = bell_draw(part_splits[3], (ITEMS, R), 0.25, 1.5, ((0, 16),), jnp.float32)
    user_noise = bell_draw(part_splits[4], (ITERS, USERS, R), 1.0, 6.0, ((1, 16),))
    item_noise = bell_draw(part_splits[5], (ITERS, ITEMS, R), 1.0, 6.0, ((1, 16),))
    return dict(rating_tiles=rating_tiles, tile_mask=tile_mask, user_rows=user_rows, item_rows=item_rows, user_noise=user_noise, item_noise=item_noise)


STEP_SIZE = 0.004

def reference(rating_tiles, tile_mask, user_rows, item_rows, user_noise, item_noise):
    noise_scale = math.sqrt(STEP_SIZE)
    blocks = ITEMS // IB
    offsets = jnp.arange(ROUNDS, dtype=jnp.int32)
    new_users = user_rows
    new_items = item_rows
    for sweep in range(ITERS):
        user_half = new_users.astype(jnp.bfloat16)
        item_half = new_items.astype(jnp.bfloat16).reshape(blocks, IB, R)

        def group_terms(group):
            start = (group * GROUP_ROWS).astype(jnp.int32)
            rows = lax.dynamic_slice_in_dim(user_half, start, GROUP_ROWS, 0).astype(jnp.float32)
            rating = lax.dynamic_slice_in_dim(rating_tiles, start, GROUP_ROWS, 0).astype(jnp.float32)
            observed = lax.dynamic_slice_in_dim(tile_mask, start, GROUP_ROWS, 0)
            visited = (group - offsets) % blocks
            factors = item_half[visited].astype(jnp.float32)
            predicted = jnp.einsum('ur,kir->uki', rows, factors)
            residual = jnp.where(observed > 0, rating - predicted, jnp.float32(0.0)).astype(jnp.bfloat16)
            resid_wide = residual.astype(jnp.float32)
            user_grad = jnp.einsum('uki,kir->ur', resid_wide, factors)
            item_part = jnp.einsum('uki,ur->kir', resid_wide, rows)
            return (user_grad, item_part)
        user_grad, item_parts = lax.map(group_terms, jnp.arange(blocks, dtype=jnp.int32))
        user_grad = user_grad.reshape(USERS, R)
        owners = (jnp.arange(blocks, dtype=jnp.int32)[:, None] - offsets[None, :]) % blocks
        item_grad = jax.ops.segment_sum(item_parts.reshape(blocks * ROUNDS, IB, R), owners.reshape(-1), num_segments=blocks).reshape(ITEMS, R)
        new_users = new_users + 0.5 * STEP_SIZE * (user_grad - new_users) + noise_scale * user_noise[sweep].astype(jnp.float32)
        new_items = new_items + 0.5 * STEP_SIZE * (item_grad - new_items) + noise_scale * item_noise[sweep].astype(jnp.float32)
    return (new_users, new_items)
```

```python
import functools
import math

import jax
import jax.numpy as jnp
from jax import lax
from jax.experimental import pallas as pl
from jax.experimental.pallas import tpu as pltpu
from jax.sharding import PartitionSpec as P

ITERS = 2

STEP_SIZE = 0.004

UNSEEN = 64.0


def nt(a, b):
    return lax.dot_general(a, b, (((1,), (1,)), ((), ())), preferred_element_type=jnp.float32)


def nn(a, b):
    return jnp.dot(a, b, preferred_element_type=jnp.float32)


def kernel(
    positions,
    rating_hbm, mask_hbm, users_hbm, items_hbm, unoise_hbm, inoise_hbm,
    out_users_hbm, out_items_hbm,
    rating_v, mask_v, users_v, items_v, unoise_v, inoise_v,
    seen_v, uhalf_v, ut_v, resid_v, block_v,
    own_v, xsend_v, xrecv_v, gsend_v, grecv_v,
    local_sem, bsend_sem, brecv_sem, fsend_sem, frecv_sem,
    xsend_sem, xrecv_sem, gsend_sem, grecv_sem,
):
    noise_scale = math.sqrt(STEP_SIZE)
    n_users, rounds, ib = rating_v.shape
    half = ib // 2
    h = lax.axis_index("blk")
    c = lax.axis_index("ugrp")
    o = 1 - c
    mine = pl.ds(pl.multiple_of(c * half, half), half)

    def ahead(d):
        return {"blk": lax.rem(h + d, positions)}

    def behind(d):
        return {"blk": lax.rem(h + positions - d, positions)}

    other = {"ugrp": o}

    loads = []
    for i, (src, dst) in enumerate((
        (items_hbm, items_v), (users_hbm, users_v), (rating_hbm, rating_v),
        (mask_hbm, mask_v), (inoise_hbm, inoise_v), (unoise_hbm, unoise_v),
    )):
        load = pltpu.make_async_copy(src, dst, local_sem.at[i])
        load.start()
        loads.append(load)

    barrier = pltpu.get_barrier_semaphore()
    peers = [other] + [ahead(d) for d in range(1, rounds)] + [behind(d) for d in range(1, rounds)]
    for peer in peers:
        pl.semaphore_signal(barrier, inc=1, device_id=peer, device_id_type=pl.DeviceIdType.MESH)
    pl.semaphore_wait(barrier, len(peers))

    def remote(src, dst, send, recv, to):
        return pltpu.make_async_remote_copy(
            src_ref=src, dst_ref=dst, send_sem=send, recv_sem=recv,
            device_id=to, device_id_type=pl.DeviceIdType.MESH,
        )

    sent = []
    loads[0].wait()
    for t in range(ITERS):
        block_v[t, 0, mine, :] = items_v[...].astype(jnp.bfloat16)
        held = block_v.at[t, 0, mine, :]
        hops = []
        for d in range(1, rounds):
            hop = remote(held, block_v.at[t, d, mine, :], bsend_sem.at[t, d], brecv_sem.at[t, d], ahead(d))
            hop.start()
            hops.append(hop)
            sent.append(hop)
        forwards = []
        for d in range(rounds):
            forwards.append(remote(
                block_v.at[t, d, mine, :], block_v.at[t, d, mine, :],
                fsend_sem.at[t, d], frecv_sem.at[t, d], other,
            ))
            sent.append(forwards[d])
        forwards[0].start()

        if t == 0:
            loads[1].wait()
        uhalf_v[...] = users_v[...].astype(jnp.bfloat16)
        ut_v[...] = uhalf_v[...].T
        if t == 0:
            loads[2].wait()
            loads[3].wait()

            @pl.loop(0, n_users // 32)
            def _(i):
                rows = pl.ds(pl.multiple_of(i * 32, 32), 32)
                seen = jnp.where(mask_v[rows] > 0, rating_v[rows].astype(jnp.float32), UNSEEN)
                seen_v[:, rows, :] = jnp.swapaxes(seen, 0, 1).astype(jnp.bfloat16)

        exchanges = []
        for d in range(rounds):
            if d + 1 < rounds:
                hops[d].wait_recv()
                forwards[d + 1].start()
            forwards[d].wait_recv()
            block = block_v[t, d]
            for r in range(0, n_users, 256):
                rows = pl.ds(r, 256)
                predicted = nt(uhalf_v[rows, :], block)
                seen = seen_v[d, rows, :].astype(jnp.float32)
                resid_v[d, rows, :] = jnp.where(seen < UNSEEN, seen - predicted, 0.0).astype(jnp.bfloat16)
            part = nn(ut_v[...], resid_v[d])
            low, high = part[:, :half], part[:, half:]
            own_v[d] = jnp.where(c == 0, low, high)
            xsend_v[t, d] = jnp.where(c == 0, high, low).astype(jnp.bfloat16)
            exchange = remote(xsend_v.at[t, d], xrecv_v.at[t, d], xsend_sem.at[t, d], xrecv_sem.at[t, d], other)
            exchange.start()
            exchanges.append(exchange)
            sent.append(exchange)
        terms = []
        for d in range(1, rounds):
            exchanges[d].wait_recv()
            gsend_v[t, d] = (own_v[d] + xrecv_v[t, d].astype(jnp.float32)).astype(jnp.bfloat16)
            term = remote(gsend_v.at[t, d], grecv_v.at[t, d], gsend_sem.at[t, d], grecv_sem.at[t, d], behind(d))
            term.start()
            terms.append(term)
            sent.append(term)

        if t == 0:
            loads[5].wait()
        for r in range(0, n_users, 256):
            rows = pl.ds(r, 256)
            grad = nn(resid_v[0, rows, :], block_v[t, 0])
            for d in range(1, rounds):
                grad = grad + nn(resid_v[d, rows, :], block_v[t, d])
            users = users_v[rows, :]
            users_v[rows, :] = (
                users + 0.5 * STEP_SIZE * (grad - users)
                + noise_scale * unoise_v[t, rows, :].astype(jnp.float32)
            )
        if t == ITERS - 1:
            put_users = pltpu.make_async_copy(users_v, out_users_hbm, local_sem.at[0])
            put_users.start()

        if t == 0:
            loads[4].wait()
        exchanges[0].wait_recv()
        total = own_v[0] + xrecv_v[t, 0].astype(jnp.float32)
        for d in range(1, rounds):
            terms[d - 1].wait_recv()
            total = total + grecv_v[t, d].astype(jnp.float32)
        items = items_v[...]
        items_v[...] = (
            items + 0.5 * STEP_SIZE * (total.T - items)
            + noise_scale * inoise_v[t].astype(jnp.float32)
        )
    put_items = pltpu.make_async_copy(items_v, out_items_hbm, local_sem.at[1])
    put_items.start()
    for copy in sent:
        copy.wait_send()
    put_users.wait()
    put_items.wait()


def per_device(rating_tiles, tile_mask, user_rows, item_rows, user_noise, item_noise):
    n_users, rounds, ib = rating_tiles.shape
    n_items, rank = item_rows.shape
    half = ib // 2
    bf16, f32 = jnp.bfloat16, jnp.float32
    dma = pltpu.SemaphoreType.DMA
    return pl.pallas_call(
        functools.partial(kernel, lax.axis_size("blk")),
        out_shape=(
            jax.ShapeDtypeStruct(user_rows.shape, f32),
            jax.ShapeDtypeStruct(item_rows.shape, f32),
        ),
        in_specs=[pl.BlockSpec(memory_space=pl.ANY)] * 6,
        out_specs=[pl.BlockSpec(memory_space=pl.ANY)] * 2,
        scratch_shapes=[
            pltpu.VMEM(rating_tiles.shape, bf16),
            pltpu.VMEM(tile_mask.shape, jnp.int32),
            pltpu.VMEM(user_rows.shape, f32),
            pltpu.VMEM(item_rows.shape, f32),
            pltpu.VMEM(user_noise.shape, bf16),
            pltpu.VMEM(item_noise.shape, bf16),
            pltpu.VMEM((rounds, n_users, ib), bf16),
            pltpu.VMEM((n_users, rank), bf16),
            pltpu.VMEM((rank, n_users), bf16),
            pltpu.VMEM((rounds, n_users, ib), bf16),
            pltpu.VMEM((ITERS, rounds, ib, rank), bf16),
            pltpu.VMEM((rounds, rank, half), f32),
            pltpu.VMEM((ITERS, rounds, rank, half), bf16),
            pltpu.VMEM((ITERS, rounds, rank, half), bf16),
            pltpu.VMEM((ITERS, rounds, rank, half), bf16),
            pltpu.VMEM((ITERS, rounds, rank, half), bf16),
            dma((6,)),
        ] + [dma((ITERS, rounds))] * 8,
        compiler_params=pltpu.CompilerParams(
            collective_id=0, has_side_effects=True, vmem_limit_bytes=60 << 20,
        ),
        cost_estimate=pl.CostEstimate(
            flops=ITERS * rounds * 6 * n_users * ib * rank, bytes_accessed=10 << 20, transcendentals=0,
        ),
    )(rating_tiles, tile_mask, user_rows, item_rows, user_noise, item_noise)


def solution(mesh):
    spec = P(("parts", "blk", "ugrp"), None)
    tiles = P(("parts", "blk", "ugrp"), None, None)
    noise = P(None, ("parts", "blk", "ugrp"), None)
    return jax.shard_map(
        per_device,
        mesh=mesh,
        in_specs=(tiles, tiles, spec, spec, noise, noise),
        out_specs=(spec, spec),
        check_vma=False,
    )
```

```python
import functools
import math

import jax
import jax.numpy as jnp
from jax import lax
from jax.experimental import pallas as pl
from jax.experimental.pallas import tpu as pltpu
from jax.sharding import PartitionSpec as P

ITERS = 2

STEP_SIZE = 0.004

PIECES = 1

UNSEEN = 64.0


def nt(a, b):
    return lax.dot_general(a, b, (((1,), (1,)), ((), ())), preferred_element_type=jnp.float32)


def nn(a, b):
    return jnp.dot(a, b, preferred_element_type=jnp.float32)


def kernel(
    positions,
    rating_hbm, mask_hbm, users_hbm, items_hbm, unoise_hbm, inoise_hbm,
    users_v, items_v,
    rating_v, mask_v, unoise_v, inoise_v,
    seen_v, uhalf_v, ut_v, resid_v, block_v,
    own_v, xsend_v, xrecv_v, gsend_v, grecv_v,
    local_sem, bsend_sem, brecv_sem, fsend_sem, frecv_sem,
    xsend_sem, xrecv_sem, gsend_sem, grecv_sem,
):
    noise_scale = math.sqrt(STEP_SIZE)
    n_users, rounds, ib = rating_v.shape
    half = ib // 2
    h = lax.axis_index("blk")
    c = lax.axis_index("ugrp")
    o = 1 - c
    mine = pl.ds(pl.multiple_of(c * half, half), half)

    def ahead(d):
        return {"blk": lax.rem(h + d, positions)}

    def behind(d):
        return {"blk": lax.rem(h + positions - d, positions)}

    other = {"ugrp": o}

    loads = []
    for i, (src, dst) in enumerate((
        (items_hbm, items_v), (users_hbm, users_v), (rating_hbm, rating_v),
        (mask_hbm, mask_v), (inoise_hbm, inoise_v), (unoise_hbm, unoise_v),
    )):
        load = pltpu.make_async_copy(src, dst, local_sem.at[i])
        load.start()
        loads.append(load)

    barrier = pltpu.get_barrier_semaphore()
    peers = [other] + [ahead(d) for d in range(1, rounds)] + [behind(d) for d in range(1, rounds)]
    for peer in peers:
        pl.semaphore_signal(barrier, inc=1, device_id=peer, device_id_type=pl.DeviceIdType.MESH)
    pl.semaphore_wait(barrier, len(peers))

    def remote(src, dst, send, recv, to):
        return pltpu.make_async_remote_copy(
            src_ref=src, dst_ref=dst, send_sem=send, recv_sem=recv,
            device_id=to, device_id_type=pl.DeviceIdType.MESH,
        )

    sent = []
    rank = items_v.shape[1]

    def spread(t, pieces, p):
        width = rank // pieces
        part = pl.ds(p * width, width)
        block_v[t, 0, mine, part] = items_v[:, part].astype(jnp.bfloat16)
        held = block_v.at[t, 0, mine, part]
        started = []
        for d in range(1, rounds):
            hop = remote(
                held, block_v.at[t, d, mine, part], bsend_sem.at[t, d, p], brecv_sem.at[t, d, p], ahead(d)
            )
            hop.start()
            started.append(hop)
            sent.append(hop)
        return started

    loads[0].wait()
    hops = [spread(0, 1, 0)]
    for t in range(ITERS):
        forwards = []
        for d in range(rounds):
            forwards.append(remote(
                block_v.at[t, d, mine, :], block_v.at[t, d, mine, :],
                fsend_sem.at[t, d], frecv_sem.at[t, d], other,
            ))
            sent.append(forwards[d])
        forwards[0].start()

        if t == 0:
            loads[1].wait()
        uhalf_v[...] = users_v[...].astype(jnp.bfloat16)
        ut_v[...] = uhalf_v[...].T
        if t == 0:
            loads[2].wait()
            loads[3].wait()

            @pl.loop(0, n_users // 32)
            def _(i):
                rows = pl.ds(pl.multiple_of(i * 32, 32), 32)
                seen = jnp.where(mask_v[rows] > 0, rating_v[rows].astype(jnp.float32), UNSEEN)
                seen_v[:, rows, :] = jnp.swapaxes(seen, 0, 1).astype(jnp.bfloat16)

        exchanges, terms = [], []

        def arrive(d):
            for piece in hops:
                piece[d - 1].wait_recv()
            forwards[d].start()

        def work(d):
            forwards[d].wait_recv()
            block = block_v[t, d]
            for r in range(0, n_users, 256):
                rows = pl.ds(r, 256)
                predicted = nt(uhalf_v[rows, :], block)
                seen = seen_v[d, rows, :].astype(jnp.float32)
                resid_v[d, rows, :] = jnp.where(seen < UNSEEN, seen - predicted, 0.0).astype(jnp.bfloat16)
            part = nn(ut_v[...], resid_v[d])
            low, high = part[:, :half], part[:, half:]
            own_v[d] = jnp.where(c == 0, low, high)
            xsend_v[t, d] = jnp.where(c == 0, high, low).astype(jnp.bfloat16)
            exchange = remote(xsend_v.at[t, d], xrecv_v.at[t, d], xsend_sem.at[t, d], xrecv_sem.at[t, d], other)
            exchange.start()
            exchanges.append(exchange)
            sent.append(exchange)

        def send(d):
            exchanges[d].wait_recv()
            gsend_v[t, d] = (own_v[d] + xrecv_v[t, d].astype(jnp.float32)).astype(jnp.bfloat16)
            started = []
            for p in range(PIECES):
                part = pl.ds(p * (rank // PIECES), rank // PIECES)
                term = remote(
                    gsend_v.at[t, d, part, :], grecv_v.at[t, d, part, :],
                    gsend_sem.at[t, d, p], grecv_sem.at[t, d, p], behind(d),
                )
                term.start()
                started.append(term)
                sent.append(term)
            terms.append(started)

        work(0)
        for d in range(1, rounds):
            arrive(d)
            if d > 1:
                send(d - 1)
            work(d)
        send(rounds - 1)

        if t == 0:
            loads[5].wait()
        for r in range(0, n_users, 256):
            rows = pl.ds(r, 256)
            grad = nn(resid_v[0, rows, :], block_v[t, 0])
            for d in range(1, rounds):
                grad = grad + nn(resid_v[d, rows, :], block_v[t, d])
            users = users_v[rows, :]
            users_v[rows, :] = (
                users + 0.5 * STEP_SIZE * (grad - users)
                + noise_scale * unoise_v[t, rows, :].astype(jnp.float32)
            )
        if t == 0:
            loads[4].wait()
        exchanges[0].wait_recv()
        hops = []
        for p in range(PIECES):
            part = pl.ds(p * (rank // PIECES), rank // PIECES)
            total = own_v[0, part, :] + xrecv_v[t, 0, part, :].astype(jnp.float32)
            for d in range(1, rounds):
                terms[d - 1][p].wait_recv()
                total = total + grecv_v[t, d, part, :].astype(jnp.float32)
            items = items_v[:, part]
            items_v[:, part] = (
                items + 0.5 * STEP_SIZE * (total.T - items)
                + noise_scale * inoise_v[t, :, part].astype(jnp.float32)
            )
            if t + 1 < ITERS:
                hops.append(spread(t + 1, PIECES, p))
    for copy in sent:
        copy.wait_send()


def write(users, items, out_users, out_items, sem):
    copies = [
        pltpu.make_async_copy(users, out_users, sem.at[0]),
        pltpu.make_async_copy(items, out_items, sem.at[1]),
    ]
    for copy in copies:
        copy.start()
    for copy in copies:
        copy.wait()


def per_device(rating_tiles, tile_mask, user_rows, item_rows, user_noise, item_noise):
    n_users, rounds, ib = rating_tiles.shape
    n_items, rank = item_rows.shape
    half = ib // 2
    bf16, f32 = jnp.bfloat16, jnp.float32
    dma = pltpu.SemaphoreType.DMA
    shapes = (
        jax.ShapeDtypeStruct(user_rows.shape, f32),
        jax.ShapeDtypeStruct(item_rows.shape, f32),
    )
    users, items = pl.pallas_call(
        functools.partial(kernel, lax.axis_size("blk")),
        out_shape=tuple(pltpu.VMEM(q.shape,q.dtype) for q in shapes),
        in_specs=[pl.BlockSpec(memory_space=pltpu.HBM)] * 6,
        out_specs=[pl.BlockSpec(memory_space=pltpu.VMEM)] * 2,
        scratch_shapes=[
            pltpu.VMEM(rating_tiles.shape, bf16),
            pltpu.VMEM(tile_mask.shape, jnp.int32),
            pltpu.VMEM(user_noise.shape, bf16),
            pltpu.VMEM(item_noise.shape, bf16),
            pltpu.VMEM((rounds, n_users, ib), bf16),
            pltpu.VMEM((n_users, rank), bf16),
            pltpu.VMEM((rank, n_users), bf16),
            pltpu.VMEM((rounds, n_users, ib), bf16),
            pltpu.VMEM((ITERS, rounds, ib, rank), bf16),
            pltpu.VMEM((rounds, rank, half), f32),
            pltpu.VMEM((ITERS, rounds, rank, half), bf16),
            pltpu.VMEM((ITERS, rounds, rank, half), bf16),
            pltpu.VMEM((ITERS, rounds, rank, half), bf16),
            pltpu.VMEM((ITERS, rounds, rank, half), bf16),
            dma((6,)),
        ] + [dma((ITERS, rounds, PIECES))] * 2 + [dma((ITERS, rounds))] * 4 + [dma((ITERS, rounds, PIECES))] * 2,
        compiler_params=pltpu.CompilerParams(
            collective_id=0, has_side_effects=True, vmem_limit_bytes=123 << 19,
        ),
        cost_estimate=pl.CostEstimate(
            flops=ITERS * rounds * 6 * n_users * ib * rank, bytes_accessed=10 << 20, transcendentals=0,
        ),
    )(rating_tiles, tile_mask, user_rows, item_rows, user_noise, item_noise)
    return pl.pallas_call(
        write,
        out_shape=shapes,
        in_specs=[pl.BlockSpec(memory_space=pl.ANY)] * 2,
        out_specs=[pl.BlockSpec(memory_space=pltpu.HBM)] * 2,
        scratch_shapes=[dma((2,))],
        compiler_params=pltpu.CompilerParams(vmem_limit_bytes=1 << 20),
    )(users, items)


def solution(mesh):
    spec = P(("parts", "blk", "ugrp"), None)
    tiles = P(("parts", "blk", "ugrp"), None, None)
    noise = P(None, ("parts", "blk", "ugrp"), None)
    return jax.shard_map(
        per_device,
        mesh=mesh,
        in_specs=(tiles, tiles, spec, spec, noise, noise),
        out_specs=(spec, spec),
        check_vma=False,
    )
```
